32 devices in a mesh: dev: 32 (over z, y, x, core).
Axes of the slice: x: 2, y: 2, z: 4, core: 2. Of those that a mesh axis runs over, the one named last changes fastest.
Arguments:
- tokens: bfloat16 [8192, 192], P('dev'), may hold values from -6 to 6
- ranges: int32 [32, 2], replicated, may hold values from 0 to 7936, as said below
- attn_in: bfloat16 [2, 110592], P(None, 'dev'), may hold values from -0.4375 to 0.4375
- attn_out: bfloat16 [2, 36864], P(None, 'dev'), may hold values from -3.5 to 3.5
- mlp_in: bfloat16 [2, 147456], P(None, 'dev'), may hold values from -0.4375 to 0.4375
- mlp_out: bfloat16 [2, 147456], P(None, 'dev'), may hold values from -0.21875 to 0.21875
- vectors: bfloat16 [2, 2304], P(None, 'dev'), may hold values from -0.75 to 1.5, as said below
- cotangent: bfloat16 [8192, 192], P('dev'), may hold values from -6 to 6
Outputs:
- activations: bfloat16 [8192, 192], P('dev')
- input_grad: float32 [8192, 192], P('dev')
- attn_in_grad: float32 [2, 110592], P(None, 'dev')
- attn_out_grad: float32 [2, 36864], P(None, 'dev')
- mlp_in_grad: float32 [2, 147456], P(None, 'dev')
- mlp_out_grad: float32 [2, 147456], P(None, 'dev')
- vectors_grad: float32 [2, 2304], P(None, 'dev')
The draws below stay inside these ranges and needn't reach their ends.
Inputs may be any that keep to these rules, and one draw needn't show every extreme that they name: Row j gives the range of stream positions on device j; ranges follow one another from 0 to 7936; each device holds 240 to 256 tokens, some device exactly 256. `vectors`: norm gains lie within 0.5 to 1.5.
All inputs are finite; a program needn't handle non-finite values.
Results may differ from the reference program's by a relative error of at most 0.01.
Values may be sent and summed in bfloat16 or wider, within the bound.
A program may use at most 64 MiB of HBM per device.

```python
import math
import jax
import jax.numpy as jnp
from jax import lax

D = 192
HEADS = 3
HD = 64
FF = 768
LAYERS = 2
IMG_LEN = 197
SLOTS = 256
SPREAD = 4
TOKENS = 7936
IMAGES = 41
N_DEV = 32


def draw_ranges(key, part):
    steps_key = jax.random.fold_in(key, 11)
    pick_key = jax.random.fold_in(key, 12)
    shifts = jax.random.randint(steps_key, (N_DEV,), -SPREAD, SPREAD + 1)
    chosen = jax.random.randint(pick_key, (), 0, N_DEV)
    positions = jnp.arange(N_DEV)
    shifts = jnp.where(positions == chosen, SPREAD, shifts)
    shifts = jnp.where(positions == (chosen - 1) % N_DEV, -SPREAD, shifts)
    lengths = SLOTS - 2 * SPREAD + shifts - jnp.roll(shifts, 1)
    ends = jnp.cumsum(lengths)
    starts = ends - lengths
    return jnp.stack([starts, ends], axis=1).astype(jnp.int32)


def draw_vectors(key, part):
    columns = 8 * D + FF
    segment = jnp.arange(columns) // D
    is_gain = (segment == 0) | (segment == 5)
    gain_key = jax.random.fold_in(key, 21)
    bias_key = jax.random.fold_in(key, 22)
    gain_part = jnp.clip(1.0 + 0.2 * jax.random.normal(gain_key, (LAYERS, columns), jnp.float32), 0.5, 1.5)
    bias_part = jnp.clip(0.3 * jax.random.normal(bias_key, (LAYERS, columns), jnp.float32), -0.75, 0.75)
    return jnp.where(is_gain[None, :], gain_part, bias_part).astype(jnp.bfloat16)


def levels(own_key, extent, shards, least, largest):
    factor_of, own = 1.0, jax.random.fold_in(own_key, 6)
    for dim, blocks in shards:
        steps = jnp.exp(jax.random.uniform(jax.random.fold_in(own, dim), (blocks,), jnp.float32, least / len(shards), largest / len(shards)))
        factor_of = factor_of * jnp.repeat(steps, extent[dim] // blocks).reshape([-1 if axis == dim else 1 for axis in range(len(extent))])
    return factor_of


def bell_draw(own_key, extent, deviation, reach, shards=(), held_as=jnp.bfloat16):
    level = levels(own_key, extent, shards, -0.22, 0.18) if shards else 1.0
    values = jax.random.normal(own_key, extent, jnp.float32) * deviation * level
    return jnp.minimum(jnp.maximum(values, -reach), reach).astype(held_as)


def setup_inputs(seed: int = 0) -> dict:
    keys = jax.random.split(jax.random.key(seed), 9)
    tokens = bell_draw(keys[0], (N_DEV * SLOTS, D), 1.0, 6.0, ((0, 32),))
    ranges = draw_ranges(jax.random.fold_in(keys[8], 71), 0)
    attn_in = bell_draw(keys[2], (LAYERS, 3 * D * D), D ** -0.5, 0.4375, ((1, 32),))
    attn_out = bell_draw(keys[3], (LAYERS, D * D), (D // 64) ** -0.5, 3.5, ((1, 32),))
    mlp_in = bell_draw(keys[4], (LAYERS, D * FF), D ** -0.5, 0.4375, ((1, 32),))
    mlp_out = bell_draw(keys[5], (LAYERS, FF * D), FF ** -0.5, 0.21875, ((1, 32),))
    vectors = draw_vectors(jax.random.fold_in(keys[8], 71), 0)
    cotangent = bell_draw(keys[7], (N_DEV * SLOTS, D), 1.0, 6.0, ((0, 32),))
    return {"tokens": tokens, "ranges": ranges, "attn_in": attn_in, "attn_out": attn_out, "mlp_in": mlp_in, "mlp_out": mlp_out, "vectors": vectors, "cotangent": cotangent}


@jax.custom_vjp
def low(v):
    return lax.optimization_barrier(v.astype(jnp.bfloat16)).astype(jnp.float32)

@jax.custom_vjp
def low_back(v):
    return v

def low_keep(v):
    return (low(v), None)

def low_pass(kept, grad):
    return (grad,)

def back_keep(v):
    return (v, None)

def back_low(kept, grad):
    return (low(grad),)
low.defvjp(low_keep, low_pass)
low_back.defvjp(back_keep, back_low)
group_images = 16
masked_fill = -1e+30

def matmul(left, right):
    return jnp.dot(left, right, precision=lax.Precision.HIGHEST)

def layer_norm(hidden, gain_vec, bias_vec):
    row_mean = lax.optimization_barrier(jnp.mean(hidden, axis=-1, keepdims=True))
    centered = hidden - row_mean
    variance = lax.optimization_barrier(jnp.mean(centered * centered, axis=-1, keepdims=True))
    return centered * lax.rsqrt(variance + 1e-06) * gain_vec + bias_vec

def block_layer(hidden, key_valid, weights):
    w_in, w_out, w_one, w_two, vector_all = weights
    ln1_gain = vector_all[0:D]
    ln1_bias = vector_all[D:2 * D]
    q_bias = vector_all[2 * D:3 * D]
    v_bias = vector_all[3 * D:4 * D]
    out_bias = vector_all[4 * D:5 * D]
    ln2_gain = vector_all[5 * D:6 * D]
    ln2_bias = vector_all[6 * D:7 * D]
    two_bias = vector_all[7 * D:8 * D]
    one_bias = vector_all[8 * D:]
    group_count, seq_len, model_width = hidden.shape
    flat_rows = hidden.reshape(group_count * seq_len, model_width)
    normed = low(layer_norm(flat_rows, ln1_gain, ln1_bias))
    projected = matmul(normed, w_in)
    queries = low_back(low(projected[:, 0:D] + q_bias)).reshape(group_count, seq_len, HEADS, HD)
    key_rows = low_back(low(projected[:, D:2 * D])).reshape(group_count, seq_len, HEADS, HD)
    values = low_back(low(projected[:, 2 * D:3 * D] + v_bias)).reshape(group_count, seq_len, HEADS, HD)
    scores = jnp.einsum('gqhd,gkhd->ghqk', queries, key_rows, precision=lax.Precision.HIGHEST) * (1.0 / math.sqrt(HD))
    scores = low_back(scores)
    scores = jnp.where(key_valid[:, None, None, :], scores, masked_fill)
    softmax_weights = jax.nn.softmax(scores, axis=-1)
    context = jnp.einsum('ghqk,gkhd->gqhd', low(softmax_weights), values, precision=lax.Precision.HIGHEST)
    context = low_back(low(context.reshape(group_count * seq_len, model_width)))
    branch_one = low_back(matmul(context, w_out) + out_bias)
    mid_stream = flat_rows + branch_one
    normed_two = low(layer_norm(mid_stream, ln2_gain, ln2_bias))
    pre_gelu = low_back(matmul(normed_two, w_one) + one_bias)
    activation = low(jax.nn.gelu(pre_gelu, approximate=False))
    branch_two = low_back(matmul(activation, w_two) + two_bias)
    return (mid_stream + branch_two).reshape(group_count, seq_len, model_width)

def reference(tokens, ranges, attn_in, attn_out, mlp_in, mlp_out, vectors, cotangent):
    group_total = -(-IMAGES // group_images)
    padded_len = group_total * group_images * IMG_LEN
    position = jnp.arange(padded_len, dtype=jnp.int32)
    starts = ranges[:, 0].astype(jnp.int32)
    ends = ranges[:, 1].astype(jnp.int32)
    owner = lax.optimization_barrier(jnp.sum((position[:, None] >= ends[None, :]).astype(jnp.int32), axis=1))
    owner = jnp.minimum(owner, N_DEV - 1).astype(jnp.int32)
    inside = position < TOKENS
    slot_index = jnp.where(inside, owner * SLOTS + position - starts[owner], 0).astype(jnp.int32)

    def forward(tokens_full, in_weights, out_weights, one_weights, two_weights, vector_rows):
        packed = tokens_full[slot_index].reshape(group_total, group_images, IMG_LEN, D)
        valid = inside.reshape(group_total, group_images, IMG_LEN)

        def run_group(payload):
            hidden, key_valid = payload
            for layer_index in range(LAYERS):
                weights = (in_weights[layer_index].reshape(D, 3 * D), out_weights[layer_index].reshape(D, D), one_weights[layer_index].reshape(D, FF), two_weights[layer_index].reshape(FF, D), vector_rows[layer_index])
                hidden = block_layer(hidden, key_valid, weights)
            return hidden
        result = lax.map(jax.checkpoint(run_group), (packed, valid))
        result = result.reshape(padded_len, D)
        result = jnp.where(inside[:, None], result, 0.0)
        return jnp.zeros((N_DEV * SLOTS, D), jnp.float32).at[slot_index].add(result)
    output, pullback = jax.vjp(forward, tokens.astype(jnp.float32), attn_in.astype(jnp.float32), attn_out.astype(jnp.float32), mlp_in.astype(jnp.float32), mlp_out.astype(jnp.float32), vectors.astype(jnp.float32))
    grads = pullback(cotangent.astype(jnp.float32))
    return (output.astype(jnp.bfloat16), grads[0], grads[1], grads[2], grads[3], grads[4], grads[5])
```

```python
import functools
import math

import jax
import jax.numpy as jnp
import numpy as np
from jax import lax
from jax.experimental import pallas as pl
from jax.experimental.pallas import tpu as pltpu
from jax.sharding import PartitionSpec as P

HD = 64
IMG_LEN = 197
ROWS = 208
IMAGES_HERE = 2
BLOCK = 16
MESH_ID = pl.DeviceIdType.MESH
bf16, f32 = jnp.bfloat16, jnp.float32
eps_norm = 1e-06
masked_fill = -1e30
vmem_bytes = 56 * 2**20


def bit_orders(n):
    count = n.bit_length() - 1
    first = list(range(count))[::-1]
    second = list(first)
    if count >= 3:
        second[-3], second[-2] = second[-2], second[-3]
    return first, second


def slot_of(dev, order, div=lax.div, rem=lax.rem):
    return sum(rem(div(dev, 2**b), 2) * 2**k for k, b in enumerate(order))


def greet(n, me, bits):
    barrier = pltpu.get_barrier_semaphore()
    others = [me + (1 - 2 * lax.rem(lax.div(me, 2**b), 2)) * 2**b for b in range(bits)]
    others += [lax.rem(me + 1, n), lax.rem(me + n - 1, n)]
    for other in others:
        pl.semaphore_signal(barrier, inc=1, device_id=(other,), device_id_type=MESH_ID)
    pl.semaphore_wait(barrier, len(others))
    return others


def remote(src, dst, send, recv, dev):
    return pltpu.make_async_remote_copy(
        src_ref=src, dst_ref=dst, send_sem=send, recv_sem=recv,
        device_id=(dev,), device_id_type=MESH_ID,
    )


def gather_kernel(n, blk_a, blk_b, halo, out_a, out_b, halo_out, send, recv, hsend, hrecv):
    me = lax.axis_index("dev")
    orders = bit_orders(n)
    bits = len(orders[0])
    outs = (out_a, out_b)
    slots = [slot_of(me, order) for order in orders]
    for half, blk in enumerate((blk_a, blk_b)):
        outs[half][pl.ds(slots[half] * BLOCK, BLOCK), :] = blk[...]
    others = greet(n, me, bits)
    halo_copy = remote(halo, halo_out, hsend, hrecv, others[-1])
    halo_copy.start()
    sent = []
    for k in range(bits):
        copies = []
        for half in range(2):
            size = BLOCK * 2**k
            at = pl.ds(pl.multiple_of(lax.div(slots[half], 2**k) * size, BLOCK), size)
            copy = remote(
                outs[half].at[at, :], outs[half].at[at, :],
                send.at[half, k], recv.at[half, k], others[orders[half][k]],
            )
            copy.start()
            copies.append(copy)
        for copy in copies:
            copy.wait_recv()
        sent += copies
    for copy in sent:
        copy.wait_send()
    halo_copy.wait()


def gather(n, blk_a, blk_b, halo):
    bits = n.bit_length() - 1
    width = blk_a.shape[1]
    vm = pl.BlockSpec(memory_space=pltpu.VMEM)
    return pl.pallas_call(
        functools.partial(gather_kernel, n),
        out_shape=(
            jax.ShapeDtypeStruct((n * BLOCK, width), bf16),
            jax.ShapeDtypeStruct((n * BLOCK, width), bf16),
            jax.ShapeDtypeStruct(halo.shape, bf16),
        ),
        in_specs=[vm] * 3,
        out_specs=(vm, vm, vm),
        scratch_shapes=[
            pltpu.SemaphoreType.DMA((2, bits)),
            pltpu.SemaphoreType.DMA((2, bits)),
            pltpu.SemaphoreType.DMA,
            pltpu.SemaphoreType.DMA,
        ],
        compiler_params=pltpu.CompilerParams(
            collective_id=0, has_side_effects=True, vmem_limit_bytes=vmem_bytes
        ),
        name="gather_params",
    )(blk_a, blk_b, halo)


def scatter_kernel(n, s_a, s_b, act, act_up, dx, dx_up,
                   r_a, r_b, act_out, dx_out, *scratch):
    me = lax.axis_index("dev")
    orders = bit_orders(n)
    bits = len(orders[0])
    inbox = [scratch[half * bits:(half + 1) * bits] for half in range(2)]
    outbox = [scratch[(2 + half) * bits:(3 + half) * bits] for half in range(2)]
    totals = [scratch[(4 + half) * bits:(5 + half) * bits] for half in range(2)]
    act_in, dx_in, send, recv, hsend, hrecv = scratch[6 * bits:]
    others = greet(n, me, bits)
    up = others[-2]
    halo = [
        remote(act_up, act_in, hsend.at[0], hrecv.at[0], up),
        remote(dx_up, dx_in, hsend.at[1], hrecv.at[1], up),
    ]
    sources = (s_a, s_b)
    copies = {}

    def bit_at(half, step):
        b = orders[half][bits - 1 - step]
        return b, lax.rem(lax.div(me, 2**b), 2)

    def start(half, step):
        b, bit = bit_at(half, step)
        size = n * BLOCK // 2 ** (step + 1)
        if step == 0:
            src = sources[half].at[pl.ds(pl.multiple_of((1 - bit) * size, BLOCK), size), :]
        else:
            src = outbox[half][step]
        copy = remote(src, inbox[half][step], send.at[half, step], recv.at[half, step], others[b])
        copy.start()
        copies[half, step] = copy

    for half in range(2):
        start(half, 0)
    for copy in halo:
        copy.start()
    for step in range(bits):
        size = n * BLOCK // 2 ** (step + 1)
        for half in range(2):
            copies[half, step].wait_recv()
            _, bit = bit_at(half, step)
            held = sources[half] if step == 0 else totals[half][step - 1]
            base = pl.multiple_of(bit * size, BLOCK)
            if step == bits - 1:
                out = (r_a, r_b)[half]
                out[...] = held[pl.ds(base, size), :].astype(f32) + inbox[half][step][...].astype(f32)
                continue
            _, next_bit = bit_at(half, step + 1)
            part = size // 2
            away = pl.multiple_of((1 - next_bit) * part, BLOCK)
            there = pl.multiple_of(next_bit * part, BLOCK)
            outbox[half][step + 1][...] = (
                held[pl.ds(base + away, part), :].astype(f32)
                + inbox[half][step][pl.ds(away, part), :].astype(f32)
            ).astype(bf16)
            start(half, step + 1)
            totals[half][step][pl.ds(there, part), :] = (
                held[pl.ds(base + there, part), :].astype(f32)
                + inbox[half][step][pl.ds(there, part), :].astype(f32)
            )
    for copy in halo:
        copy.wait_recv()
    act_out[...] = act[...] + act_in[...]
    dx_out[...] = dx[...] + dx_in[...]
    for copy in halo + list(copies.values()):
        copy.wait_send()


def scatter(n, s_a, s_b, act, act_up, dx, dx_up):
    bits = n.bit_length() - 1
    width = s_a.shape[1]
    vm = pl.BlockSpec(memory_space=pltpu.VMEM)
    sizes = [n * BLOCK // 2 ** (step + 1) for step in range(bits)]
    boxes = [pltpu.VMEM((size, width), bf16) for size in sizes]
    totals = [pltpu.VMEM((size, width), f32) for size in sizes]
    return pl.pallas_call(
        functools.partial(scatter_kernel, n),
        out_shape=(
            jax.ShapeDtypeStruct((BLOCK, width), f32),
            jax.ShapeDtypeStruct((BLOCK, width), f32),
            jax.ShapeDtypeStruct(act.shape, act.dtype),
            jax.ShapeDtypeStruct(dx.shape, dx.dtype),
        ),
        in_specs=[vm] * 6,
        out_specs=(vm,) * 4,
        scratch_shapes=boxes * 4 + totals * 2 + [
            pltpu.VMEM(act.shape, act.dtype),
            pltpu.VMEM(dx.shape, dx.dtype),
            pltpu.SemaphoreType.DMA((2, bits)),
            pltpu.SemaphoreType.DMA((2, bits)),
            pltpu.SemaphoreType.DMA((2,)),
            pltpu.SemaphoreType.DMA((2,)),
        ],
        compiler_params=pltpu.CompilerParams(
            collective_id=1, has_side_effects=True, vmem_limit_bytes=vmem_bytes
        ),
        name="scatter_grads",
    )(s_a, s_b, act, act_up, dx, dx_up)


def mm(a, b):
    return jnp.dot(a, b, preferred_element_type=f32)


def mm_nt(a, b):
    return lax.dot_general(a, b, (((1,), (1,)), ((), ())), preferred_element_type=f32)


def mm_tn(a, b):
    return lax.dot_general(a, b, (((0,), (0,)), ((), ())), preferred_element_type=f32)


def norm_forward(x, gain, bias):
    centered = x - jnp.mean(x, axis=-1, keepdims=True)
    inverse = lax.rsqrt(jnp.mean(centered * centered, axis=-1, keepdims=True) + eps_norm)
    hat = centered * inverse
    return (hat * gain + bias).astype(bf16), hat, inverse


def norm_backward(dh, hat, inverse, gain):
    scaled = dh * gain
    dv = inverse * (
        scaled
        - jnp.mean(scaled, axis=-1, keepdims=True)
        - hat * jnp.mean(scaled * hat, axis=-1, keepdims=True)
    )
    return dv, rows_sum(dh * hat), rows_sum(dh)


def rows_sum(x):
    return jnp.sum(x, axis=0, keepdims=True)


def compute_kernel(n, fast, layers, width, hidden_units, ranges, *refs):
    refs = list(refs)
    take = lambda count: [refs.pop(0) for _ in range(count)]
    if fast:
        g_a, g_b, place, perm = take(4)
    else:
        w_full, perm = take(2)
    tok, cot, halo = take(3)
    if fast:
        s_a, s_b = take(2)
    else:
        (grad_out,) = take(1)
    act_own, act_up, dx_own, dx_up = take(4)
    w_all, w_one_s, w_two_s, hat1_s, h1_s, qkv_s, p_s, o_s, hat2_s, h2_s, slope_s, a_s = take(12)
    inv_s, dqkv_s, do_s, grad_s = take(4)
    slots = tok.shape[0]
    heads = width // HD
    d = width
    half_width = 6 * d
    me = lax.axis_index("dev")
    first, last = ranges[me, 0], ranges[me, 1]
    total = ranges[n - 1, 1]
    image = (first + IMG_LEN - 1) // IMG_LEN
    rows = IMAGES_HERE * ROWS

    picks, valid_keys = [], []
    for k in range(IMAGES_HERE):
        begin = (image + k) * IMG_LEN
        count = jnp.where(begin < last, jnp.minimum(IMG_LEN, total - begin), 0)
        r = lax.broadcasted_iota(jnp.int32, (ROWS, 2 * slots), 0)
        c = lax.broadcasted_iota(jnp.int32, (ROWS, 2 * slots), 1)
        t = begin + r
        column = jnp.where(t < last, t - first, t - last + slots)
        column = jnp.where(r < count, column, -1)
        picks.append(jnp.where(column == c, 1.0, 0.0).astype(bf16))
        valid_keys.append(lax.broadcasted_iota(jnp.int32, (ROWS, ROWS), 1) < count)
    pick = jnp.concatenate(picks, axis=0)
    x = mm(pick[:, :slots], tok[...]) + mm(pick[:, slots:], halo[:, :d])

    vec = [None] * layers
    b_one = [None] * layers
    for l in range(layers):
        if fast:
            w_all[l, :, :half_width] = mm(place[0, l], g_a[...]).astype(bf16)
            w_all[l, :, half_width:] = mm(place[1, l], g_b[...]).astype(bf16)
        else:
            w_all[l] = w_full[l]
        w_one_s[l] = mm(w_all[l, :d, 4 * d:8 * d], perm[...]).astype(bf16)
        for j in range(4):
            w_two_s[l, j * d:(j + 1) * d, :] = w_all[l, :d, (8 + j) * d:(9 + j) * d]
        tail = w_all[l, d:d + BLOCK, :]
        vec[l] = tail.astype(f32)[0:1, :]
        b_one[l] = mm(tail[:, 8 * d:], perm[...])[0:1, :]

    def v_of(l, index):
        return vec[l][:, index * d:(index + 1) * d]

    for l in range(layers):
        h, hat, inv = norm_forward(x, v_of(l, 0), v_of(l, 1))
        hat1_s[l], h1_s[l], inv_s[l, 0] = hat, h, inv
        projected = mm(h, w_all[l, :d, :3 * d])
        qkv_s[l, :, :d] = ((projected[:, :d] + v_of(l, 2)).astype(bf16).astype(f32)
                           * (1.0 / math.sqrt(HD))).astype(bf16)
        qkv_s[l, :, d:2 * d] = projected[:, d:2 * d].astype(bf16)
        qkv_s[l, :, 2 * d:] = (projected[:, 2 * d:] + v_of(l, 3)).astype(bf16)
        for i in range(IMAGES_HERE):
            at = slice(i * ROWS, (i + 1) * ROWS)
            for head in range(heads):
                q = qkv_s[l, at, head * HD:(head + 1) * HD]
                key = qkv_s[l, at, d + head * HD:d + (head + 1) * HD]
                val = qkv_s[l, at, 2 * d + head * HD:2 * d + (head + 1) * HD]
                scores = jnp.where(valid_keys[i], mm_nt(q, key), masked_fill)
                e = jnp.exp(scores - jnp.max(scores, axis=-1, keepdims=True))
                p = e * (1.0 / jnp.sum(e, axis=-1, keepdims=True))
                p_s[l, i, head] = p
                o_s[l, at, head * HD:(head + 1) * HD] = mm(p.astype(bf16), val).astype(bf16)
        x1 = x + (mm(o_s[l], w_all[l, :d, 3 * d:4 * d]) + v_of(l, 4))
        h2, hat, inv = norm_forward(x1, v_of(l, 5), v_of(l, 6))
        hat2_s[l], h2_s[l], inv_s[l, 1] = hat, h2, inv
        u = mm(h2, w_one_s[l]) + b_one[l]
        phi = 0.5 * (1.0 + lax.erf(u * (1.0 / math.sqrt(2.0))))
        a_s[l] = (u * phi).astype(bf16)
        slope_s[l] = phi + u * (jnp.exp(-0.5 * u * u) * (1.0 / math.sqrt(2.0 * math.pi)))
        x = x1 + (mm(a_s[l], w_two_s[l]) + v_of(l, 7))

    x_low = x.astype(bf16)
    act_own[...] = mm_tn(pick[:, :slots], x_low).astype(bf16)
    act_up[...] = mm_tn(pick[:, slots:], x_low).astype(bf16)

    dx = mm(pick[:, :slots], cot[...]) + mm(pick[:, slots:], halo[:, d:])
    for l in reversed(range(layers)):
        dm = dx.astype(bf16)
        g_two = mm_tn(a_s[l], dm)
        for j in range(4):
            grad_s[l, :d, (8 + j) * d:(9 + j) * d] = g_two[j * d:(j + 1) * d, :].astype(bf16)
        g_b2 = rows_sum(dm.astype(f32))
        du = (mm_nt(dm, w_two_s[l]) * slope_s[l]).astype(bf16)
        g_b1 = mm_nt(jnp.broadcast_to(rows_sum(du.astype(f32)), (BLOCK, hidden_units)).astype(bf16),
                     perm[...])[0:1, :]
        g_one = mm_tn(h2_s[l], du).astype(bf16)
        grad_s[l, :d, 4 * d:8 * d] = mm_nt(g_one, perm[...]).astype(bf16)
        dh2 = mm_nt(du, w_one_s[l])
        dv, g_g2, g_c2 = norm_backward(dh2, hat2_s[l], inv_s[l, 1], v_of(l, 5))
        dx1 = dx + dv
        db = dx1.astype(bf16)
        g_bo = rows_sum(db.astype(f32))
        grad_s[l, :d, 3 * d:4 * d] = mm_tn(o_s[l], db).astype(bf16)
        do_s[...] = mm_nt(db, w_all[l, :d, 3 * d:4 * d]).astype(bf16)
        for i in range(IMAGES_HERE):
            at = slice(i * ROWS, (i + 1) * ROWS)
            for head in range(heads):
                q_at = slice(head * HD, (head + 1) * HD)
                k_at = slice(d + head * HD, d + (head + 1) * HD)
                v_at = slice(2 * d + head * HD, 2 * d + (head + 1) * HD)
                do = do_s[at, q_at]
                p = p_s[l, i, head]
                dp = mm_nt(do, qkv_s[l, at, v_at])
                ds = (p * (dp - jnp.sum(p * dp, axis=-1, keepdims=True))).astype(bf16)
                dqkv_s[at, q_at] = (mm(ds, qkv_s[l, at, k_at]) * (1.0 / math.sqrt(HD))).astype(bf16)
                dqkv_s[at, k_at] = mm_tn(ds, qkv_s[l, at, q_at]).astype(bf16)
                dqkv_s[at, v_at] = mm_tn(p.astype(bf16), do).astype(bf16)
        g_bq = rows_sum(dqkv_s[:, :d].astype(f32))
        g_bv = rows_sum(dqkv_s[:, 2 * d:].astype(f32))
        grad_s[l, :d, :3 * d] = mm_tn(h1_s[l], dqkv_s[...]).astype(bf16)
        dh = mm_nt(dqkv_s[...], w_all[l, :d, :3 * d])
        dv, g_g1, g_c1 = norm_backward(dh, hat1_s[l], inv_s[l, 0], v_of(l, 0))
        dx = dx1 + dv
        line = jnp.concatenate([g_g1, g_c1, g_bq, g_bv, g_bo, g_g2, g_c2, g_b2, g_b1], axis=1)
        grad_s[l, d:d + BLOCK, :] = jnp.broadcast_to(line, (BLOCK, line.shape[1])).astype(bf16)

    high = dx.astype(bf16)
    low = (dx - high.astype(f32)).astype(bf16)
    dx_own[...] = mm_tn(pick[:, :slots], high) + mm_tn(pick[:, :slots], low)
    dx_up[...] = mm_tn(pick[:, slots:], high) + mm_tn(pick[:, slots:], low)
    if fast:
        for half, out in enumerate((s_a, s_b)):
            cols = slice(half * half_width, (half + 1) * half_width)
            part = mm_tn(place[half, 0], grad_s[0, :, cols])
            for l in range(1, layers):
                part += mm_tn(place[half, l], grad_s[l, :, cols])
            out[...] = part.astype(bf16)
    else:
        grad_out[...] = grad_s[...]


def compute(n, fast, ranges, weights, tok, cot, halo, layers):
    slots, d = tok.shape
    hidden_units = 4 * d
    rows = IMAGES_HERE * ROWS
    tall = d + BLOCK
    wide = 12 * d
    unit = np.arange(hidden_units)
    perm = np.zeros((hidden_units, hidden_units), np.float32)
    perm[unit, (unit % 4) * d + unit // 4] = 1.0
    args = list(weights)
    if fast:
        per = d // n
        place = np.zeros((2, layers, tall, n * BLOCK), np.float32)
        for half, order in enumerate(bit_orders(n)):
            for dev in range(n):
                at = slot_of(dev, order, lambda a, b: a // b, lambda a, b: a % b) * BLOCK
                for l in range(layers):
                    for i in range(per):
                        place[half, l, dev * per + i, at + l * per + i] = 1.0
                    place[half, l, d, at + layers * per + l] = 1.0
        args.append(jnp.asarray(place, bf16))
        outs = [jax.ShapeDtypeStruct((n * BLOCK, wide // 2), bf16)] * 2
    else:
        outs = [jax.ShapeDtypeStruct((layers, tall, wide), bf16)]
    args += [jnp.asarray(perm, bf16), tok, cot, halo]
    outs += [jax.ShapeDtypeStruct((slots, d), bf16)] * 2 + [jax.ShapeDtypeStruct((slots, d), f32)] * 2
    vm = pl.BlockSpec(memory_space=pltpu.VMEM)
    return pl.pallas_call(
        functools.partial(compute_kernel, n, fast, layers, d, hidden_units),
        out_shape=tuple(outs),
        in_specs=[pl.BlockSpec(memory_space=pltpu.SMEM)] + [vm] * len(args),
        out_specs=(vm,) * len(outs),
        scratch_shapes=[
            pltpu.VMEM((layers, tall, wide), bf16),
            pltpu.VMEM((layers, d, hidden_units), bf16),
            pltpu.VMEM((layers, hidden_units, d), bf16),
            pltpu.VMEM((layers, rows, d), f32),
            pltpu.VMEM((layers, rows, d), bf16),
            pltpu.VMEM((layers, rows, 3 * d), bf16),
            pltpu.VMEM((layers, IMAGES_HERE, d // HD, ROWS, ROWS), f32),
            pltpu.VMEM((layers, rows, d), bf16),
            pltpu.VMEM((layers, rows, d), f32),
            pltpu.VMEM((layers, rows, d), bf16),
            pltpu.VMEM((layers, rows, hidden_units), f32),
            pltpu.VMEM((layers, rows, hidden_units), bf16),
            pltpu.VMEM((layers, 2, rows, 1), f32),
            pltpu.VMEM((rows, 3 * d), bf16),
            pltpu.VMEM((rows, d), bf16),
            pltpu.VMEM((layers, tall, wide), bf16),
        ],
        compiler_params=pltpu.CompilerParams(vmem_limit_bytes=vmem_bytes),
        name="two_layers",
    )(ranges, *args)


def rows_of(flats, d):
    w_in, w_out, w_one, w_two = flats
    layers = w_in.shape[0]
    return jnp.concatenate(
        [
            w_in.reshape(layers, -1, 3 * d),
            w_out.reshape(layers, -1, d),
            w_one.reshape(layers, -1, 4 * d),
            w_two.reshape(layers, -1, 4 * d),
        ],
        axis=2,
    )


def flats_of(block, d):
    layers = block.shape[0]
    ends = (0, 3 * d, 4 * d, 8 * d, 12 * d)
    return [block[:, :, lo:hi].reshape(layers, -1) for lo, hi in zip(ends, ends[1:])]


def local(tokens, ranges, attn_in, attn_out, mlp_in, mlp_out, vectors, cotangent):
    n = lax.axis_size("dev")
    me = lax.axis_index("dev")
    slots, d = tokens.shape
    layers, part = vectors.shape
    flats = (attn_in, attn_out, mlp_in, mlp_out)
    halo = jnp.concatenate([tokens, cotangent], axis=1)
    fast = d % n == 0 and n & (n - 1) == 0 and layers * (d // n + 1) <= BLOCK and n >= 8
    if fast:
        per = d // n
        block = rows_of(flats, d).reshape(layers * per, 12 * d)
        line = jnp.zeros((layers, 12 * d), bf16)
        line = lax.dynamic_update_slice(line, vectors, (0, me * part))
        spare = jnp.zeros((BLOCK - layers * (per + 1), 12 * d), bf16)
        block = jnp.concatenate([block, line, spare], axis=0)
        g_a, g_b, halo_in = gather(n, block[:, :6 * d], block[:, 6 * d:], halo)
        s_a, s_b, act, act_up, dx, dx_up = compute(
            n, True, ranges, (g_a, g_b), tokens, cotangent, halo_in, layers
        )
        r_a, r_b, act, dx = scatter(n, s_a, s_b, act, act_up, dx, dx_up)
        full = jnp.concatenate([r_a, r_b], axis=1)
        grads = flats_of(full[:layers * per].reshape(layers, per, 12 * d), d)
        lines = full[layers * per:layers * (per + 1)]
        grads.append(lax.dynamic_slice(lines, (0, me * part), (layers, part)))
    else:
        whole = [
            jnp.stack([lax.all_gather(flat[l], "dev", axis=0, tiled=True) for l in range(layers)])
            for flat in flats + (vectors,)
        ]
        line = whole.pop()
        spare = jnp.zeros((layers, BLOCK - 1, 12 * d), bf16)
        block = jnp.concatenate([rows_of(whole, d), line[:, None, :], spare], axis=1)
        halo_in = lax.ppermute(halo, "dev", [(i, (i + n - 1) % n) for i in range(n)])
        grad, act, act_up, dx, dx_up = compute(
            n, False, ranges, (block,), tokens, cotangent, halo_in, layers
        )
        up = [(i, (i + 1) % n) for i in range(n)]
        act = act + lax.ppermute(act_up, "dev", up)
        dx = dx + lax.ppermute(dx_up, "dev", up)
        terms = flats_of(grad[:, :d], d) + [grad[:, d]]
        grads = [
            jnp.stack([
                lax.psum_scatter(term[l].astype(f32), "dev", scatter_dimension=0, tiled=True)
                for l in range(layers)
            ])
            for term in terms
        ]
    return (act, dx, *grads)


def solution(mesh):
    flat = P(None, "dev")
    rows = P("dev", None)
    return jax.shard_map(
        local,
        mesh=mesh,
        in_specs=(rows, P(), flat, flat, flat, flat, flat, rows),
        out_specs=(rows, rows, flat, flat, flat, flat, flat),
        check_vma=False,
    )
```

```python
import functools
import math

import jax
import jax.numpy as jnp
from jax import lax
from jax.experimental import pallas as pl
from jax.experimental.pallas import tpu as pltpu
from jax.sharding import PartitionSpec as P

HD = 64
IMG_LEN = 197
ROWS = 208
IMAGES_HERE = 2
BLOCK = 16
MESH_ID = pl.DeviceIdType.MESH
bf16, f32 = jnp.bfloat16, jnp.float32
eps_norm = 1e-06
masked_fill = -1e30
vmem_bytes = 56 * 2**20


PIECES = 6


def bit_orders(n):
    down = list(range(n.bit_length() - 1))[::-1]
    lead, (p, q, r, s) = down[:-4], down[-4:]
    first, second = lead + [p, q, r, s], lead + [p, r, q, s]
    third, fourth = lead + [q, r, p, s], lead + [r, q, p, s]
    return first, second, third, first, second, fourth


def slot_of(dev, order, div=lax.div, rem=lax.rem):
    return sum(rem(div(dev, 2**b), 2) * 2**k for k, b in enumerate(order))


def greet(n, me, bits):
    barrier = pltpu.get_barrier_semaphore()
    others = [me + (1 - 2 * lax.rem(lax.div(me, 2**b), 2)) * 2**b for b in range(bits)]
    others += [lax.rem(me + 1, n), lax.rem(me + n - 1, n)]
    for other in others:
        pl.semaphore_signal(barrier, inc=1, device_id=(other,), device_id_type=MESH_ID)
    pl.semaphore_wait(barrier, len(others))
    return others


def remote(src, dst, send, recv, dev):
    return pltpu.make_async_remote_copy(
        src_ref=src, dst_ref=dst, send_sem=send, recv_sem=recv,
        device_id=(dev,), device_id_type=MESH_ID,
    )


def gather_kernel(n, blk, tok, cot, *refs):
    outs, (tok_out, cot_out, send, recv, hsend, hrecv) = refs[:PIECES], refs[PIECES:]
    me = lax.axis_index("dev")
    orders = bit_orders(n)
    bits = len(orders[0])
    slots = [slot_of(me, order) for order in orders]
    width = outs[0].shape[1]
    for c in range(PIECES):
        outs[c][pl.ds(slots[c] * BLOCK, BLOCK), :] = blk[:, c * width:(c + 1) * width]
    others = greet(n, me, bits)
    sent = []
    for k in range(bits):
        copies = []
        for c in range(PIECES):
            if k:
                sent[-PIECES].wait_recv()
            size = BLOCK * 2**k
            at = pl.ds(pl.multiple_of(lax.div(slots[c], 2**k) * size, BLOCK), size)
            copy = remote(
                outs[c].at[at, :], outs[c].at[at, :],
                send.at[c, k], recv.at[c, k], others[orders[c][k]],
            )
            copy.start()
            sent.append(copy)
        if k == 0:
            halo = [
                remote(tok, tok_out, hsend.at[0], hrecv.at[0], others[-1]),
                remote(cot, cot_out, hsend.at[1], hrecv.at[1], others[-1]),
            ]
            for copy in halo:
                copy.start()
    for copy in sent[-PIECES:]:
        copy.wait_recv()
    for copy in sent:
        copy.wait_send()
    for copy in halo:
        copy.wait()


def gather(n, blk, tok, cot):
    bits = n.bit_length() - 1
    width = blk.shape[1] // PIECES
    vm = pl.BlockSpec(memory_space=pltpu.VMEM)
    return pl.pallas_call(
        functools.partial(gather_kernel, n),
        out_shape=(jax.ShapeDtypeStruct((n * BLOCK, width), bf16),) * PIECES
        + (jax.ShapeDtypeStruct(tok.shape, bf16),) * 2,
        in_specs=[vm] * 3,
        out_specs=(vm,) * (PIECES + 2),
        scratch_shapes=[
            pltpu.SemaphoreType.DMA((PIECES, bits)),
            pltpu.SemaphoreType.DMA((PIECES, bits)),
            pltpu.SemaphoreType.DMA((2,)),
            pltpu.SemaphoreType.DMA((2,)),
        ],
        compiler_params=pltpu.CompilerParams(
            collective_id=0, has_side_effects=True, vmem_limit_bytes=vmem_bytes
        ),
        name="gather_params",
    )(blk, tok, cot)


def scatter_kernel(n, *refs):
    sources, refs = refs[:PIECES], refs[PIECES:]
    act, act_up, dx, dx_up, result, act_out, dx_out = refs[:7]
    scratch = refs[7:]
    me = lax.axis_index("dev")
    orders = bit_orders(n)
    bits = len(orders[0])
    width = sources[0].shape[1]
    groups = [scratch[k * bits:(k + 1) * bits] for k in range(3 * PIECES)]
    inbox, outbox, totals = groups[:PIECES], groups[PIECES:2 * PIECES], groups[2 * PIECES:]
    act_in, dx_in, send, recv, hsend, hrecv = scratch[3 * PIECES * bits:]
    others = greet(n, me, bits)
    up = others[-2]
    halo = [
        remote(act_up, act_in, hsend.at[0], hrecv.at[0], up),
        remote(dx_up, dx_in, hsend.at[1], hrecv.at[1], up),
    ]
    copies = {}

    def bit_at(half, step):
        b = orders[half][bits - 1 - step]
        return b, lax.rem(lax.div(me, 2**b), 2)

    def start(half, step):
        b, bit = bit_at(half, step)
        size = n * BLOCK // 2 ** (step + 1)
        if step == 0:
            src = sources[half].at[pl.ds(pl.multiple_of((1 - bit) * size, BLOCK), size), :]
        else:
            src = outbox[half][step]
        copy = remote(src, inbox[half][step], send.at[half, step], recv.at[half, step], others[b])
        copy.start()
        copies[half, step] = copy

    for half in range(PIECES):
        start(half, 0)
    for copy in halo:
        copy.start()
    for step in range(bits):
        size = n * BLOCK // 2 ** (step + 1)
        for half in range(PIECES):
            copies[half, step].wait_recv()
            _, bit = bit_at(half, step)
            held = sources[half] if step == 0 else totals[half][step - 1]
            base = pl.multiple_of(bit * size, BLOCK)
            if step == bits - 1:
                result[:, half * width:(half + 1) * width] = held[pl.ds(base, size), :].astype(f32) + inbox[half][step][...].astype(f32)
                continue
            _, next_bit = bit_at(half, step + 1)
            part = size // 2
            away = pl.multiple_of((1 - next_bit) * part, BLOCK)
            there = pl.multiple_of(next_bit * part, BLOCK)
            outbox[half][step + 1][...] = (
                held[pl.ds(base + away, part), :].astype(f32)
                + inbox[half][step][pl.ds(away, part), :].astype(f32)
            ).astype(bf16)
            start(half, step + 1)
            totals[half][step][pl.ds(there, part), :] = (
                held[pl.ds(base + there, part), :].astype(f32)
                + inbox[half][step][pl.ds(there, part), :].astype(f32)
            )
    for copy in halo:
        copy.wait_recv()
    act_out[...] = act[...] + act_in[...]
    dx_out[...] = dx[...] + dx_in[...]
    for copy in halo + list(copies.values()):
        copy.wait_send()


def scatter(n, parts, act, act_up, dx, dx_up):
    bits = n.bit_length() - 1
    width = parts[0].shape[1]
    vm = pl.BlockSpec(memory_space=pltpu.VMEM)
    sizes = [n * BLOCK // 2 ** (step + 1) for step in range(bits)]
    boxes = [pltpu.VMEM((size, width), bf16) for size in sizes]
    totals = [pltpu.VMEM((size, width), f32) for size in sizes]
    return pl.pallas_call(
        functools.partial(scatter_kernel, n),
        out_shape=(
            jax.ShapeDtypeStruct((BLOCK, PIECES * width), f32),
            jax.ShapeDtypeStruct(act.shape, act.dtype),
            jax.ShapeDtypeStruct(dx.shape, dx.dtype),
        ),
        in_specs=[vm] * (PIECES + 4),
        out_specs=(vm,) * 3,
        scratch_shapes=boxes * (2 * PIECES) + totals * PIECES + [
            pltpu.VMEM(act.shape, act.dtype),
            pltpu.VMEM(dx.shape, dx.dtype),
            pltpu.SemaphoreType.DMA((PIECES, bits)),
            pltpu.SemaphoreType.DMA((PIECES, bits)),
            pltpu.SemaphoreType.DMA((2,)),
            pltpu.SemaphoreType.DMA((2,)),
        ],
        compiler_params=pltpu.CompilerParams(
            collective_id=1, has_side_effects=True, vmem_limit_bytes=vmem_bytes
        ),
        name="scatter_grads",
    )(*parts, act, act_up, dx, dx_up)


def mm(a, b):
    return jnp.dot(a, b, preferred_element_type=f32)


def mm_nt(a, b):
    return lax.dot_general(a, b, (((1,), (1,)), ((), ())), preferred_element_type=f32)


def mm_tn(a, b):
    return lax.dot_general(a, b, (((0,), (0,)), ((), ())), preferred_element_type=f32)


def norm_forward(x, gain, bias):
    centered = x - jnp.mean(x, axis=-1, keepdims=True)
    inverse = lax.rsqrt(jnp.mean(centered * centered, axis=-1, keepdims=True) + eps_norm)
    hat = centered * inverse
    return (hat * gain + bias).astype(bf16), hat, inverse


def norm_backward(dh, hat, inverse, gain):
    scaled = dh * gain
    dv = inverse * (
        scaled
        - jnp.mean(scaled, axis=-1, keepdims=True)
        - hat * jnp.mean(scaled * hat, axis=-1, keepdims=True)
    )
    return dv, rows_sum(dh * hat), rows_sum(dh)


def rows_sum(x):
    return jnp.sum(x, axis=0, keepdims=True)


def compute_kernel(n, fast, layers, width, hidden_units, ranges, *refs):
    refs = list(refs)
    take = lambda count: [refs.pop(0) for _ in range(count)]
    if fast:
        pieces = take(PIECES)
    else:
        (w_full,) = take(1)
    tok, cot, tok_up, cot_up = take(4)
    if fast:
        parts = take(PIECES)
    else:
        (grad_out,) = take(1)
    act_own, act_up, dx_own, dx_up = take(4)
    w_all, w_one_s, w_two_s, hat1_s, h1_s, qkv_s, p_s, o_s, hat2_s, h2_s, slope_s, a_s = take(12)
    inv_s, dqkv_s, do_s, grad_s, perm = take(5)
    slots = tok.shape[0]
    heads = width // HD
    d = width
    me = lax.axis_index("dev")
    first, last = ranges[me, 0], ranges[me, 1]
    total = ranges[n - 1, 1]
    image = (first + IMG_LEN - 1) // IMG_LEN
    rows = IMAGES_HERE * ROWS

    picks, valid_keys = [], []
    for k in range(IMAGES_HERE):
        begin = (image + k) * IMG_LEN
        count = jnp.where(begin < last, jnp.minimum(IMG_LEN, total - begin), 0)
        r = lax.broadcasted_iota(jnp.int32, (ROWS, 2 * slots), 0)
        c = lax.broadcasted_iota(jnp.int32, (ROWS, 2 * slots), 1)
        t = begin + r
        column = jnp.where(t < last, t - first, t - last + slots)
        column = jnp.where(r < count, column, -1)
        picks.append(jnp.where(column == c, 1.0, 0.0).astype(bf16))
        valid_keys.append(lax.broadcasted_iota(jnp.int32, (ROWS, ROWS), 1) < count)
    pick = jnp.concatenate(picks, axis=0)
    x = mm(pick[:, :slots], tok[...]) + mm(pick[:, slots:], tok_up[...])

    unit = lax.broadcasted_iota(jnp.int32, (1, hidden_units), 1)
    group = sum(jnp.where(unit >= j * d, 1, 0) for j in range(1, 4))
    origin = 4 * (unit - group * d) + group
    f = lax.broadcasted_iota(jnp.int32, (hidden_units, hidden_units), 0)
    perm[...] = jnp.where(f == origin, 1.0, 0.0).astype(bf16)
    if fast:
        (place_s,) = take(1)
        per = d // n
        orders = bit_orders(n)
        kinds = [orders[:c + 1].index(order) for c, order in enumerate(orders)]
        c = lax.broadcasted_iota(jnp.int32, (1, n * BLOCK), 1)
        line = lax.broadcasted_iota(jnp.int32, (d + BLOCK, n * BLOCK), 0)
        inside = c & (BLOCK - 1)
        for kind in set(kinds):
            dev = sum(((c >> (4 + k)) & 1) << b for k, b in enumerate(orders[kind]))
            for l in range(layers):
                row = inside - l * per
                goal = jnp.where((row >= 0) & (row < per), dev * per + row, -1)
                goal = jnp.where(inside == layers * per + l, d, goal)
                place_s[kind, l] = jnp.where(line == goal, 1.0, 0.0).astype(bf16)

    vec = [None] * layers
    b_one = [None] * layers
    for l in range(layers):
        if fast:
            for c, piece in enumerate(pieces):
                cols = slice(c * piece.shape[1], (c + 1) * piece.shape[1])
                w_all[l, :, cols] = mm(place_s[kinds[c], l], piece[...]).astype(bf16)
        else:
            w_all[l] = w_full[l]
        w_one_s[l] = mm(w_all[l, :d, 4 * d:8 * d], perm[...]).astype(bf16)
        for j in range(4):
            w_two_s[l, j * d:(j + 1) * d, :] = w_all[l, :d, (8 + j) * d:(9 + j) * d]
        tail = w_all[l, d:d + BLOCK, :]
        vec[l] = tail.astype(f32)[0:1, :]
        b_one[l] = mm(tail[:, 8 * d:], perm[...])[0:1, :]

    def v_of(l, index):
        return vec[l][:, index * d:(index + 1) * d]

    for l in range(layers):
        h, hat, inv = norm_forward(x, v_of(l, 0), v_of(l, 1))
        hat1_s[l], h1_s[l], inv_s[l, 0] = hat, h, inv
        projected = mm(h, w_all[l, :d, :3 * d])
        qkv_s[l, :, :d] = ((projected[:, :d] + v_of(l, 2)).astype(bf16).astype(f32)
                           * (1.0 / math.sqrt(HD))).astype(bf16)
        qkv_s[l, :, d:2 * d] = projected[:, d:2 * d].astype(bf16)
        qkv_s[l, :, 2 * d:] = (projected[:, 2 * d:] + v_of(l, 3)).astype(bf16)
        for i in range(IMAGES_HERE):
            at = slice(i * ROWS, (i + 1) * ROWS)
            for head in range(heads):
                q = qkv_s[l, at, head * HD:(head + 1) * HD]
                key = qkv_s[l, at, d + head * HD:d + (head + 1) * HD]
                val = qkv_s[l, at, 2 * d + head * HD:2 * d + (head + 1) * HD]
                scores = jnp.where(valid_keys[i], mm_nt(q, key), masked_fill)
                e = jnp.exp(scores - jnp.max(scores, axis=-1, keepdims=True))
                p = e * (1.0 / jnp.sum(e, axis=-1, keepdims=True))
                p_s[l, i, head] = p
                o_s[l, at, head * HD:(head + 1) * HD] = mm(p.astype(bf16), val).astype(bf16)
        x1 = x + (mm(o_s[l], w_all[l, :d, 3 * d:4 * d]) + v_of(l, 4))
        h2, hat, inv = norm_forward(x1, v_of(l, 5), v_of(l, 6))
        hat2_s[l], h2_s[l], inv_s[l, 1] = hat, h2, inv
        u = mm(h2, w_one_s[l]) + b_one[l]
        phi = 0.5 * (1.0 + lax.erf(u * (1.0 / math.sqrt(2.0))))
        a_s[l] = (u * phi).astype(bf16)
        slope_s[l] = phi + u * (jnp.exp(-0.5 * u * u) * (1.0 / math.sqrt(2.0 * math.pi)))
        x = x1 + (mm(a_s[l], w_two_s[l]) + v_of(l, 7))

    x_low = x.astype(bf16)
    act_own[...] = mm_tn(pick[:, :slots], x_low).astype(bf16)
    act_up[...] = mm_tn(pick[:, slots:], x_low).astype(bf16)

    dx = mm(pick[:, :slots], cot[...]) + mm(pick[:, slots:], cot_up[...])
    for l in reversed(range(layers)):
        dm = dx.astype(bf16)
        g_two = mm_tn(a_s[l], dm)
        for j in range(4):
            grad_s[l, :d, (8 + j) * d:(9 + j) * d] = g_two[j * d:(j + 1) * d, :].astype(bf16)
        g_b2 = rows_sum(dm.astype(f32))
        du = (mm_nt(dm, w_two_s[l]) * slope_s[l]).astype(bf16)
        g_b1 = mm_nt(jnp.broadcast_to(rows_sum(du.astype(f32)), (BLOCK, hidden_units)).astype(bf16),
                     perm[...])[0:1, :]
        g_one = mm_tn(h2_s[l], du).astype(bf16)
        grad_s[l, :d, 4 * d:8 * d] = mm_nt(g_one, perm[...]).astype(bf16)
        dh2 = mm_nt(du, w_one_s[l])
        dv, g_g2, g_c2 = norm_backward(dh2, hat2_s[l], inv_s[l, 1], v_of(l, 5))
        dx1 = dx + dv
        db = dx1.astype(bf16)
        g_bo = rows_sum(db.astype(f32))
        grad_s[l, :d, 3 * d:4 * d] = mm_tn(o_s[l], db).astype(bf16)
        do_s[...] = mm_nt(db, w_all[l, :d, 3 * d:4 * d]).astype(bf16)
        for i in range(IMAGES_HERE):
            at = slice(i * ROWS, (i + 1) * ROWS)
            for head in range(heads):
                q_at = slice(head * HD, (head + 1) * HD)
                k_at = slice(d + head * HD, d + (head + 1) * HD)
                v_at = slice(2 * d + head * HD, 2 * d + (head + 1) * HD)
                do = do_s[at, q_at]
                p = p_s[l, i, head]
                dp = mm_nt(do, qkv_s[l, at, v_at])
                ds = (p * (dp - jnp.sum(p * dp, axis=-1, keepdims=True))).astype(bf16)
                dqkv_s[at, q_at] = (mm(ds, qkv_s[l, at, k_at]) * (1.0 / math.sqrt(HD))).astype(bf16)
                dqkv_s[at, k_at] = mm_tn(ds, qkv_s[l, at, q_at]).astype(bf16)
                dqkv_s[at, v_at] = mm_tn(p.astype(bf16), do).astype(bf16)
        g_bq = rows_sum(dqkv_s[:, :d].astype(f32))
        g_bv = rows_sum(dqkv_s[:, 2 * d:].astype(f32))
        grad_s[l, :d, :3 * d] = mm_tn(h1_s[l], dqkv_s[...]).astype(bf16)
        dh = mm_nt(dqkv_s[...], w_all[l, :d, :3 * d])
        dv, g_g1, g_c1 = norm_backward(dh, hat1_s[l], inv_s[l, 0], v_of(l, 0))
        dx = dx1 + dv
        line = jnp.concatenate([g_g1, g_c1, g_bq, g_bv, g_bo, g_g2, g_c2, g_b2, g_b1], axis=1)
        grad_s[l, d:d + BLOCK, :] = jnp.broadcast_to(line, (BLOCK, line.shape[1])).astype(bf16)

    high = dx.astype(bf16)
    low = (dx - high.astype(f32)).astype(bf16)
    dx_own[...] = mm_tn(pick[:, :slots], high) + mm_tn(pick[:, :slots], low)
    dx_up[...] = mm_tn(pick[:, slots:], high) + mm_tn(pick[:, slots:], low)
    if fast:
        for c, out in enumerate(parts):
            cols = slice(c * out.shape[1], (c + 1) * out.shape[1])
            part = mm_tn(place_s[kinds[c], 0], grad_s[0, :, cols])
            for l in range(1, layers):
                part += mm_tn(place_s[kinds[c], l], grad_s[l, :, cols])
            out[...] = part.astype(bf16)
    else:
        grad_out[...] = grad_s[...]


def compute(n, fast, ranges, weights, tok, cot, tok_up, cot_up, layers):
    slots, d = tok.shape
    hidden_units = 4 * d
    rows = IMAGES_HERE * ROWS
    tall = d + BLOCK
    wide = 12 * d
    args = list(weights) + [tok, cot, tok_up, cot_up]
    if fast:
        outs = [jax.ShapeDtypeStruct((n * BLOCK, wide // PIECES), bf16)] * PIECES
        place = [pltpu.VMEM((PIECES, layers, tall, n * BLOCK), bf16)]
    else:
        outs = [jax.ShapeDtypeStruct((layers, tall, wide), bf16)]
        place = []
    outs += [jax.ShapeDtypeStruct((slots, d), bf16)] * 2 + [jax.ShapeDtypeStruct((slots, d), f32)] * 2
    vm = pl.BlockSpec(memory_space=pltpu.VMEM)
    return pl.pallas_call(
        functools.partial(compute_kernel, n, fast, layers, d, hidden_units),
        out_shape=tuple(outs),
        in_specs=[pl.BlockSpec(memory_space=pltpu.SMEM)] + [vm] * len(args),
        out_specs=(vm,) * len(outs),
        scratch_shapes=[
            pltpu.VMEM((layers, tall, wide), bf16),
            pltpu.VMEM((layers, d, hidden_units), bf16),
            pltpu.VMEM((layers, hidden_units, d), bf16),
            pltpu.VMEM((layers, rows, d), f32),
            pltpu.VMEM((layers, rows, d), bf16),
            pltpu.VMEM((layers, rows, 3 * d), bf16),
            pltpu.VMEM((layers, IMAGES_HERE, d // HD, ROWS, ROWS), f32),
            pltpu.VMEM((layers, rows, d), bf16),
            pltpu.VMEM((layers, rows, d), f32),
            pltpu.VMEM((layers, rows, d), bf16),
            pltpu.VMEM((layers, rows, hidden_units), f32),
            pltpu.VMEM((layers, rows, hidden_units), bf16),
            pltpu.VMEM((layers, 2, rows, 1), f32),
            pltpu.VMEM((rows, 3 * d), bf16),
            pltpu.VMEM((rows, d), bf16),
            pltpu.VMEM((layers, tall, wide), bf16),
            pltpu.VMEM((hidden_units, hidden_units), bf16),
        ] + place,
        compiler_params=pltpu.CompilerParams(vmem_limit_bytes=vmem_bytes),
        name="two_layers",
    )(ranges, *args)


def rows_of(flats, d):
    w_in, w_out, w_one, w_two = flats
    layers = w_in.shape[0]
    return jnp.concatenate(
        [
            w_in.reshape(layers, -1, 3 * d),
            w_out.reshape(layers, -1, d),
            w_one.reshape(layers, -1, 4 * d),
            w_two.reshape(layers, -1, 4 * d),
        ],
        axis=2,
    )


def flats_of(block, d):
    layers = block.shape[0]
    ends = (0, 3 * d, 4 * d, 8 * d, 12 * d)
    return [block[:, :, lo:hi].reshape(layers, -1) for lo, hi in zip(ends, ends[1:])]


def local(tokens, ranges, attn_in, attn_out, mlp_in, mlp_out, vectors, cotangent):
    n = lax.axis_size("dev")
    me = lax.axis_index("dev")
    slots, d = tokens.shape
    layers, part = vectors.shape
    flats = (attn_in, attn_out, mlp_in, mlp_out)
    fast = d % n == 0 and n & (n - 1) == 0 and layers * (d // n + 1) <= BLOCK and n >= 32
    if fast:
        per = d // n
        block = rows_of(flats, d).reshape(layers * per, 12 * d)
        line = jnp.zeros((layers, 12 * d), bf16)
        line = lax.dynamic_update_slice(line, vectors, (0, me * part))
        spare = jnp.zeros((BLOCK - layers * (per + 1), 12 * d), bf16)
        block = jnp.concatenate([block, line, spare], axis=0)
        *pieces, tok_up, cot_up = gather(n, block, tokens, cotangent)
        *parts, act, act_up, dx, dx_up = compute(
            n, True, ranges, pieces, tokens, cotangent, tok_up, cot_up, layers
        )
        full, act, dx = scatter(n, parts, act, act_up, dx, dx_up)
        grads = flats_of(full[:layers * per].reshape(layers, per, 12 * d), d)
        lines = full[layers * per:layers * (per + 1)]
        grads.append(lax.dynamic_slice(lines, (0, me * part), (layers, part)))
    else:
        whole = [
            jnp.stack([lax.all_gather(flat[l], "dev", axis=0, tiled=True) for l in range(layers)])
            for flat in flats + (vectors,)
        ]
        line = whole.pop()
        spare = jnp.zeros((layers, BLOCK - 1, 12 * d), bf16)
        block = jnp.concatenate([rows_of(whole, d), line[:, None, :], spare], axis=1)
        down = [(i, (i + n - 1) % n) for i in range(n)]
        tok_up, cot_up = lax.ppermute(tokens, "dev", down), lax.ppermute(cotangent, "dev", down)
        grad, act, act_up, dx, dx_up = compute(
            n, False, ranges, (block,), tokens, cotangent, tok_up, cot_up, layers
        )
        up = [(i, (i + 1) % n) for i in range(n)]
        act = act + lax.ppermute(act_up, "dev", up)
        dx = dx + lax.ppermute(dx_up, "dev", up)
        terms = flats_of(grad[:, :d], d) + [grad[:, d]]
        grads = [
            jnp.stack([
                lax.psum_scatter(term[l].astype(f32), "dev", scatter_dimension=0, tiled=True)
                for l in range(layers)
            ])
            for term in terms
        ]
    return (act, dx, *grads)


def solution(mesh):
    flat = P(None, "dev")
    rows = P("dev", None)
    return jax.shard_map(
        local,
        mesh=mesh,
        in_specs=(rows, P(), flat, flat, flat, flat, flat, rows),
        out_specs=(rows, rows, flat, flat, flat, flat, flat),
        check_vma=False,
    )
```

```python
import functools
import math

import jax
import jax.numpy as jnp
from jax import lax
from jax.experimental import pallas as pl
from jax.experimental.pallas import tpu as pltpu
from jax.sharding import PartitionSpec as P

HD = 64
IMG_LEN = 197
ROWS = 208
IMAGES_HERE = 2
BLOCK = 16
MESH_ID = pl.DeviceIdType.MESH
bf16, f32 = jnp.bfloat16, jnp.float32
eps_norm = 1e-06
masked_fill = -1e30
vmem_bytes = 56 * 2**20


PIECES = 6


def bit_orders(n):
    down = list(range(n.bit_length() - 1))[::-1]
    lead, (p, q, r, s) = down[:-4], down[-4:]
    first, second = lead + [p, q, r, s], lead + [p, r, q, s]
    third, fourth = lead + [q, r, p, s], lead + [r, q, p, s]
    return first, second, third, first, second, fourth


def slot_of(dev, order, div=lax.div, rem=lax.rem):
    return sum(rem(div(dev, 2**b), 2) * 2**k for k, b in enumerate(order))


def greet(n, me, bits):
    barrier = pltpu.get_barrier_semaphore()
    others = [me + (1 - 2 * lax.rem(lax.div(me, 2**b), 2)) * 2**b for b in range(bits)]
    others += [lax.rem(me + 1, n), lax.rem(me + n - 1, n)]
    for other in others:
        pl.semaphore_signal(barrier, inc=1, device_id=(other,), device_id_type=MESH_ID)
    pl.semaphore_wait(barrier, len(others))
    return others


def remote(src, dst, send, recv, dev):
    return pltpu.make_async_remote_copy(
        src_ref=src, dst_ref=dst, send_sem=send, recv_sem=recv,
        device_id=(dev,), device_id_type=MESH_ID,
    )


def gather_kernel(n, blk, tok, cot, *refs):
    outs, (tok_out, cot_out, send, recv, hsend, hrecv) = refs[:PIECES], refs[PIECES:]
    me = lax.axis_index("dev")
    orders = bit_orders(n)
    bits = len(orders[0])
    slots = [slot_of(me, order) for order in orders]
    width = outs[0].shape[1]
    for c in range(PIECES):
        outs[c][pl.ds(slots[c] * BLOCK, BLOCK), :] = blk[:, c * width:(c + 1) * width]
    others = greet(n, me, bits)
    sent = []
    for k in range(bits):
        copies = []
        for c in range(PIECES):
            if k:
                sent[-PIECES].wait_recv()
            size = BLOCK * 2**k
            at = pl.ds(pl.multiple_of(lax.div(slots[c], 2**k) * size, BLOCK), size)
            copy = remote(
                outs[c].at[at, :], outs[c].at[at, :],
                send.at[c, k], recv.at[c, k], others[orders[c][k]],
            )
            copy.start()
            sent.append(copy)
        if k == 0:
            halo = [
                remote(tok, tok_out, hsend.at[0], hrecv.at[0], others[-1]),
                remote(cot, cot_out, hsend.at[1], hrecv.at[1], others[-1]),
            ]
            for copy in halo:
                copy.start()
    for copy in sent[-PIECES:]:
        copy.wait_recv()
    for copy in sent:
        copy.wait_send()
    for copy in halo:
        copy.wait()


def gather(n, blk, tok, cot):
    bits = n.bit_length() - 1
    width = blk.shape[1] // PIECES
    vm = pl.BlockSpec(memory_space=pltpu.VMEM)
    return pl.pallas_call(
        functools.partial(gather_kernel, n),
        out_shape=(jax.ShapeDtypeStruct((n * BLOCK, width), bf16),) * PIECES
        + (jax.ShapeDtypeStruct(tok.shape, bf16),) * 2,
        in_specs=[vm] + [pl.BlockSpec(memory_space=pl.ANY)] * 2,
        out_specs=(vm,) * (PIECES + 2),
        scratch_shapes=[
            pltpu.SemaphoreType.DMA((PIECES, bits)),
            pltpu.SemaphoreType.DMA((PIECES, bits)),
            pltpu.SemaphoreType.DMA((2,)),
            pltpu.SemaphoreType.DMA((2,)),
        ],
        compiler_params=pltpu.CompilerParams(
            collective_id=0, has_side_effects=True, vmem_limit_bytes=vmem_bytes
        ),
        name="gather_params",
    )(blk, tok, cot)


def scatter_kernel(n, *refs):
    sources, refs = refs[:PIECES], refs[PIECES:]
    act, act_up, dx, dx_up, result, act_out, dx_out = refs[:7]
    scratch = refs[7:]
    me = lax.axis_index("dev")
    orders = bit_orders(n)
    bits = len(orders[0])
    width = sources[0].shape[1]
    groups = [scratch[k * bits:(k + 1) * bits] for k in range(3 * PIECES)]
    inbox, outbox, totals = groups[:PIECES], groups[PIECES:2 * PIECES], groups[2 * PIECES:]
    act_in, dx_in, send, recv, hsend, hrecv = scratch[3 * PIECES * bits:]
    others = greet(n, me, bits)
    up = others[-2]
    halo = [
        remote(act_up, act_in, hsend.at[0], hrecv.at[0], up),
        remote(dx_up, dx_in, hsend.at[1], hrecv.at[1], up),
    ]
    copies = {}

    def bit_at(half, step):
        b = orders[half][bits - 1 - step]
        return b, lax.rem(lax.div(me, 2**b), 2)

    def start(half, step):
        b, bit = bit_at(half, step)
        size = n * BLOCK // 2 ** (step + 1)
        if step == 0:
            src = sources[half].at[pl.ds(pl.multiple_of((1 - bit) * size, BLOCK), size), :]
        else:
            src = outbox[half][step]
        copy = remote(src, inbox[half][step], send.at[half, step], recv.at[half, step], others[b])
        copy.start()
        copies[half, step] = copy

    for half in range(PIECES):
        start(half, 0)
    for copy in halo:
        copy.start()
    for step in range(bits):
        size = n * BLOCK // 2 ** (step + 1)
        for half in range(PIECES):
            copies[half, step].wait_recv()
            _, bit = bit_at(half, step)
            held = sources[half] if step == 0 else totals[half][step - 1]
            base = pl.multiple_of(bit * size, BLOCK)
            if step == bits - 1:
                result[:, half * width:(half + 1) * width] = held[pl.ds(base, size), :].astype(f32) + inbox[half][step][...].astype(f32)
                continue
            _, next_bit = bit_at(half, step + 1)
            part = size // 2
            away = pl.multiple_of((1 - next_bit) * part, BLOCK)
            there = pl.multiple_of(next_bit * part, BLOCK)
            outbox[half][step + 1][...] = (
                held[pl.ds(base + away, part), :].astype(f32)
                + inbox[half][step][pl.ds(away, part), :].astype(f32)
            ).astype(bf16)
            start(half, step + 1)
            totals[half][step][pl.ds(there, part), :] = (
                held[pl.ds(base + there, part), :].astype(f32)
                + inbox[half][step][pl.ds(there, part), :].astype(f32)
            )
    for copy in halo:
        copy.wait_recv()
    act_out[...] = act[...] + act_in[...]
    dx_out[...] = dx[...] + dx_in[...].astype(f32)
    for copy in halo + list(copies.values()):
        copy.wait_send()


def scatter(n, parts, act, act_up, dx, dx_up):
    bits = n.bit_length() - 1
    width = parts[0].shape[1]
    vm = pl.BlockSpec(memory_space=pltpu.VMEM)
    sizes = [n * BLOCK // 2 ** (step + 1) for step in range(bits)]
    boxes = [pltpu.VMEM((size, width), bf16) for size in sizes]
    totals = [pltpu.VMEM((size, width), f32) for size in sizes]
    return pl.pallas_call(
        functools.partial(scatter_kernel, n),
        out_shape=(
            jax.ShapeDtypeStruct((BLOCK, PIECES * width), f32),
            jax.ShapeDtypeStruct(act.shape, act.dtype),
            jax.ShapeDtypeStruct(dx.shape, dx.dtype),
        ),
        in_specs=[vm] * (PIECES + 4),
        out_specs=(vm,) * 3,
        scratch_shapes=boxes * (2 * PIECES) + totals * PIECES + [
            pltpu.VMEM(act.shape, act.dtype),
            pltpu.VMEM(dx.shape, bf16),
            pltpu.SemaphoreType.DMA((PIECES, bits)),
            pltpu.SemaphoreType.DMA((PIECES, bits)),
            pltpu.SemaphoreType.DMA((2,)),
            pltpu.SemaphoreType.DMA((2,)),
        ],
        compiler_params=pltpu.CompilerParams(
            collective_id=1, has_side_effects=True, vmem_limit_bytes=vmem_bytes
        ),
        name="scatter_grads",
    )(*parts, act, act_up, dx, dx_up)


def mm(a, b):
    return jnp.dot(a, b, preferred_element_type=f32)


def mm_nt(a, b):
    return lax.dot_general(a, b, (((1,), (1,)), ((), ())), preferred_element_type=f32)


def mm_tn(a, b):
    return lax.dot_general(a, b, (((0,), (0,)), ((), ())), preferred_element_type=f32)


def norm_forward(x, gain, bias):
    centered = x - jnp.mean(x, axis=-1, keepdims=True)
    inverse = lax.rsqrt(jnp.mean(centered * centered, axis=-1, keepdims=True) + eps_norm)
    hat = centered * inverse
    return (hat * gain + bias).astype(bf16), hat, inverse


def norm_backward(dh, hat, inverse, gain):
    scaled = dh * gain
    dv = inverse * (
        scaled
        - jnp.mean(scaled, axis=-1, keepdims=True)
        - hat * jnp.mean(scaled * hat, axis=-1, keepdims=True)
    )
    return dv, rows_sum(dh * hat), rows_sum(dh)


def rows_sum(x):
    return jnp.sum(x, axis=0, keepdims=True)


def goal_of(c, order, per, layers, l, d):
    inside = c & (BLOCK - 1)
    dev = sum(((c >> (4 + k)) & 1) << b for k, b in enumerate(order))
    row = inside - l * per
    goal = jnp.where((row >= 0) & (row < per), dev * per + row, -1)
    return jnp.where(inside == layers * per + l, d, goal)


def compute_kernel(n, fast, layers, width, hidden_units, ranges, *refs):
    refs = list(refs)
    take = lambda count: [refs.pop(0) for _ in range(count)]
    if fast:
        pieces = take(PIECES)
    else:
        (w_full,) = take(1)
    tok, cot, tok_up, cot_up = take(4)
    if fast:
        parts = take(PIECES)
    else:
        (grad_out,) = take(1)
    act_own, act_up, dx_own, dx_up = take(4)
    w_all, w_one_s, w_two_s, hat1_s, h1_s, qkv_s, p_s, o_s, hat2_s, h2_s, slope_s, a_s = take(12)
    inv_s, dqkv_s, do_s, grad_s, perm = take(5)
    slots = tok.shape[1]
    heads = width // HD
    d = width
    me = lax.axis_index("dev")
    first, last = ranges[me, 0], ranges[me, 1]
    total = ranges[n - 1, 1]
    image = (first + IMG_LEN - 1) // IMG_LEN
    rows = IMAGES_HERE * ROWS

    picks, valid_keys = [], []
    for k in range(IMAGES_HERE):
        begin = (image + k) * IMG_LEN
        count = jnp.where(begin < last, jnp.minimum(IMG_LEN, total - begin), 0)
        r = lax.broadcasted_iota(jnp.int32, (ROWS, 2 * slots), 0)
        c = lax.broadcasted_iota(jnp.int32, (ROWS, 2 * slots), 1)
        t = begin + r
        column = jnp.where(t < last, t - first, t - last + slots)
        column = jnp.where(r < count, column, -1)
        picks.append(jnp.where(column == c, 1.0, 0.0).astype(bf16))
        valid_keys.append(lax.broadcasted_iota(jnp.int32, (ROWS, ROWS), 1) < count)
    pick = jnp.concatenate(picks, axis=0)
    x = mm_nt(pick[:, :slots], tok[...]) + mm_nt(pick[:, slots:], tok_up[...])

    unit = lax.broadcasted_iota(jnp.int32, (1, hidden_units), 1)
    group = sum(jnp.where(unit >= j * d, 1, 0) for j in range(1, 4))
    origin = 4 * (unit - group * d) + group
    f = lax.broadcasted_iota(jnp.int32, (hidden_units, hidden_units), 0)
    perm[...] = jnp.where(f == origin, 1.0, 0.0).astype(bf16)
    if fast:
        place_s, back_s = take(2)
        per = d // n
        orders = bit_orders(n)
        kinds = [orders[:c + 1].index(order) for c, order in enumerate(orders)]
        c = lax.broadcasted_iota(jnp.int32, (1, n * BLOCK), 1)
        line = lax.broadcasted_iota(jnp.int32, (d + BLOCK, n * BLOCK), 0)
        c_down = lax.broadcasted_iota(jnp.int32, (n * BLOCK, 1), 0)
        line_across = lax.broadcasted_iota(jnp.int32, (n * BLOCK, d + BLOCK), 1)
        for kind in sorted(set(kinds)):
            for l in range(layers):
                goal = goal_of(c_down, orders[kind], per, layers, l, d)
                back_s[kind, l] = jnp.where(line_across == goal, 1.0, 0.0).astype(bf16)
                goal = goal_of(c, orders[kind], per, layers, l, d)
                place_s[kind, l] = jnp.where(line == goal, 1.0, 0.0).astype(bf16)

    vec = [None] * layers
    b_one = [None] * layers
    for l in range(layers):
        if fast:
            for c, piece in enumerate(pieces):
                cols = slice(c * piece.shape[1], (c + 1) * piece.shape[1])
                w_all[l, :, cols] = mm(place_s[kinds[c], l], piece[...]).astype(bf16)
        else:
            w_all[l] = w_full[l]
        w_one_s[l] = mm(w_all[l, :d, 4 * d:8 * d], perm[...]).astype(bf16)
        for j in range(4):
            w_two_s[l, j * d:(j + 1) * d, :] = w_all[l, :d, (8 + j) * d:(9 + j) * d]
        tail = w_all[l, d:d + BLOCK, :]
        vec[l] = tail.astype(f32)[0:1, :]
        b_one[l] = mm(tail[:, 8 * d:], perm[...])[0:1, :]

    def v_of(l, index):
        return vec[l][:, index * d:(index + 1) * d]

    for l in range(layers):
        h, hat, inv = norm_forward(x, v_of(l, 0), v_of(l, 1))
        hat1_s[l], h1_s[l], inv_s[l, 0] = hat, h, inv
        projected = mm(h, w_all[l, :d, :3 * d])
        qkv_s[l, :, :d] = ((projected[:, :d] + v_of(l, 2)).astype(bf16).astype(f32)
                           * (1.0 / math.sqrt(HD))).astype(bf16)
        qkv_s[l, :, d:2 * d] = projected[:, d:2 * d].astype(bf16)
        qkv_s[l, :, 2 * d:] = (projected[:, 2 * d:] + v_of(l, 3)).astype(bf16)
        for i in range(IMAGES_HERE):
            at = slice(i * ROWS, (i + 1) * ROWS)
            for head in range(heads):
                q = qkv_s[l, at, head * HD:(head + 1) * HD]
                key = qkv_s[l, at, d + head * HD:d + (head + 1) * HD]
                val = qkv_s[l, at, 2 * d + head * HD:2 * d + (head + 1) * HD]
                scores = jnp.where(valid_keys[i], mm_nt(q, key), masked_fill)
                e = jnp.exp(scores - jnp.max(scores, axis=-1, keepdims=True))
                p = e * (1.0 / jnp.sum(e, axis=-1, keepdims=True))
                p_s[l, i, head] = p
                o_s[l, at, head * HD:(head + 1) * HD] = mm(p.astype(bf16), val).astype(bf16)
        x1 = x + (mm(o_s[l], w_all[l, :d, 3 * d:4 * d]) + v_of(l, 4))
        h2, hat, inv = norm_forward(x1, v_of(l, 5), v_of(l, 6))
        hat2_s[l], h2_s[l], inv_s[l, 1] = hat, h2, inv
        u = mm(h2, w_one_s[l]) + b_one[l]
        phi = 0.5 * (1.0 + lax.erf(u * (1.0 / math.sqrt(2.0))))
        a_s[l] = (u * phi).astype(bf16)
        slope_s[l] = phi + u * (jnp.exp(-0.5 * u * u) * (1.0 / math.sqrt(2.0 * math.pi)))
        x = x1 + (mm(a_s[l], w_two_s[l]) + v_of(l, 7))

    x_low = x.astype(bf16)
    act_own[...] = mm_tn(x_low, pick[:, :slots]).astype(bf16)
    act_up[...] = mm_tn(x_low, pick[:, slots:]).astype(bf16)

    dx = mm_nt(pick[:, :slots], cot[...]) + mm_nt(pick[:, slots:], cot_up[...])
    for l in reversed(range(layers)):
        dm = dx.astype(bf16)
        g_two = mm_tn(a_s[l], dm)
        for j in range(4):
            grad_s[l, :d, (8 + j) * d:(9 + j) * d] = g_two[j * d:(j + 1) * d, :].astype(bf16)
        g_b2 = rows_sum(dm.astype(f32))
        du = (mm_nt(dm, w_two_s[l]) * slope_s[l]).astype(bf16)
        g_b1 = mm_nt(jnp.broadcast_to(rows_sum(du.astype(f32)), (BLOCK, hidden_units)).astype(bf16),
                     perm[...])[0:1, :]
        g_one = mm_tn(h2_s[l], du).astype(bf16)
        grad_s[l, :d, 4 * d:8 * d] = mm_nt(g_one, perm[...]).astype(bf16)
        dh2 = mm_nt(du, w_one_s[l])
        dv, g_g2, g_c2 = norm_backward(dh2, hat2_s[l], inv_s[l, 1], v_of(l, 5))
        dx1 = dx + dv
        db = dx1.astype(bf16)
        g_bo = rows_sum(db.astype(f32))
        grad_s[l, :d, 3 * d:4 * d] = mm_tn(o_s[l], db).astype(bf16)
        do_s[...] = mm_nt(db, w_all[l, :d, 3 * d:4 * d]).astype(bf16)
        for i in range(IMAGES_HERE):
            at = slice(i * ROWS, (i + 1) * ROWS)
            for head in range(heads):
                q_at = slice(head * HD, (head + 1) * HD)
                k_at = slice(d + head * HD, d + (head + 1) * HD)
                v_at = slice(2 * d + head * HD, 2 * d + (head + 1) * HD)
                do = do_s[at, q_at]
                p = p_s[l, i, head]
                dp = mm_nt(do, qkv_s[l, at, v_at])
                ds = (p * (dp - jnp.sum(p * dp, axis=-1, keepdims=True))).astype(bf16)
                dqkv_s[at, q_at] = (mm(ds, qkv_s[l, at, k_at]) * (1.0 / math.sqrt(HD))).astype(bf16)
                dqkv_s[at, k_at] = mm_tn(ds, qkv_s[l, at, q_at]).astype(bf16)
                dqkv_s[at, v_at] = mm_tn(p.astype(bf16), do).astype(bf16)
        g_bq = rows_sum(dqkv_s[:, :d].astype(f32))
        g_bv = rows_sum(dqkv_s[:, 2 * d:].astype(f32))
        grad_s[l, :d, :3 * d] = mm_tn(h1_s[l], dqkv_s[...]).astype(bf16)
        dh = mm_nt(dqkv_s[...], w_all[l, :d, :3 * d])
        dv, g_g1, g_c1 = norm_backward(dh, hat1_s[l], inv_s[l, 0], v_of(l, 0))
        dx = dx1 + dv
        line = jnp.concatenate([g_g1, g_c1, g_bq, g_bv, g_bo, g_g2, g_c2, g_b2, g_b1], axis=1)
        grad_s[l, d:d + BLOCK, :] = jnp.broadcast_to(line, (BLOCK, line.shape[1])).astype(bf16)

    high = dx.astype(bf16)
    low = (dx - high.astype(f32)).astype(bf16)
    dx_own[...] = mm_tn(high, pick[:, :slots]) + mm_tn(low, pick[:, :slots])
    dx_up[...] = mm_tn(high, pick[:, slots:]).astype(bf16)
    if fast:
        for c, out in enumerate(parts):
            cols = slice(c * out.shape[1], (c + 1) * out.shape[1])
            part = mm(back_s[kinds[c], 0], grad_s[0, :, cols])
            for l in range(1, layers):
                part += mm(back_s[kinds[c], l], grad_s[l, :, cols])
            out[...] = part.astype(bf16)
    else:
        grad_out[...] = grad_s[...]


def compute(n, fast, ranges, weights, tok, cot, tok_up, cot_up, layers):
    d, slots = tok.shape
    hidden_units = 4 * d
    rows = IMAGES_HERE * ROWS
    tall = d + BLOCK
    wide = 12 * d
    args = list(weights) + [tok, cot, tok_up, cot_up]
    if fast:
        outs = [jax.ShapeDtypeStruct((n * BLOCK, wide // PIECES), bf16)] * PIECES
        place = [
            pltpu.VMEM((PIECES, layers, tall, n * BLOCK), bf16),
            pltpu.VMEM((PIECES, layers, n * BLOCK, tall), bf16),
        ]
    else:
        outs = [jax.ShapeDtypeStruct((layers, tall, wide), bf16)]
        place = []
    outs += [
        jax.ShapeDtypeStruct((d, slots), kind) for kind in (bf16, bf16, f32, bf16)
    ]
    vm = pl.BlockSpec(memory_space=pltpu.VMEM)
    return pl.pallas_call(
        functools.partial(compute_kernel, n, fast, layers, d, hidden_units),
        out_shape=tuple(outs),
        in_specs=[pl.BlockSpec(memory_space=pltpu.SMEM)] + [vm] * len(args),
        out_specs=(vm,) * len(outs),
        scratch_shapes=[
            pltpu.VMEM((layers, tall, wide), bf16),
            pltpu.VMEM((layers, d, hidden_units), bf16),
            pltpu.VMEM((layers, hidden_units, d), bf16),
            pltpu.VMEM((layers, rows, d), f32),
            pltpu.VMEM((layers, rows, d), bf16),
            pltpu.VMEM((layers, rows, 3 * d), bf16),
            pltpu.VMEM((layers, IMAGES_HERE, d // HD, ROWS, ROWS), f32),
            pltpu.VMEM((layers, rows, d), bf16),
            pltpu.VMEM((layers, rows, d), f32),
            pltpu.VMEM((layers, rows, d), bf16),
            pltpu.VMEM((layers, rows, hidden_units), f32),
            pltpu.VMEM((layers, rows, hidden_units), bf16),
            pltpu.VMEM((layers, 2, rows, 1), f32),
            pltpu.VMEM((rows, 3 * d), bf16),
            pltpu.VMEM((rows, d), bf16),
            pltpu.VMEM((layers, tall, wide), bf16),
            pltpu.VMEM((hidden_units, hidden_units), bf16),
        ] + place,
        compiler_params=pltpu.CompilerParams(vmem_limit_bytes=vmem_bytes),
        name="two_layers",
    )(ranges, *args)


def rows_of(flats, d):
    w_in, w_out, w_one, w_two = flats
    layers = w_in.shape[0]
    return jnp.concatenate(
        [
            w_in.reshape(layers, -1, 3 * d),
            w_out.reshape(layers, -1, d),
            w_one.reshape(layers, -1, 4 * d),
            w_two.reshape(layers, -1, 4 * d),
        ],
        axis=2,
    )


def flats_of(block, d):
    layers = block.shape[0]
    ends = (0, 3 * d, 4 * d, 8 * d, 12 * d)
    return [block[:, :, lo:hi].reshape(layers, -1) for lo, hi in zip(ends, ends[1:])]


def local(tokens, ranges, attn_in, attn_out, mlp_in, mlp_out, vectors, cotangent):
    n = lax.axis_size("dev")
    me = lax.axis_index("dev")
    slots, d = tokens.shape
    layers, part = vectors.shape
    tokens, cotangent = tokens.T, cotangent.T
    flats = (attn_in, attn_out, mlp_in, mlp_out)
    fast = d % n == 0 and n & (n - 1) == 0 and layers * (d // n + 1) <= BLOCK and n >= 32
    if fast:
        per = d // n
        block = rows_of(flats, d).reshape(layers * per, 12 * d)
        line = jnp.zeros((layers, 12 * d), bf16)
        line = lax.dynamic_update_slice(line, vectors, (0, me * part))
        spare = jnp.zeros((BLOCK - layers * (per + 1), 12 * d), bf16)
        block = jnp.concatenate([block, line, spare], axis=0)
        *pieces, tok_up, cot_up = gather(n, block, tokens, cotangent)
        *parts, act, act_up, dx, dx_up = compute(
            n, True, ranges, pieces, tokens, cotangent, tok_up, cot_up, layers
        )
        full, act, dx = scatter(n, parts, act, act_up, dx, dx_up)
        grads = flats_of(full[:layers * per].reshape(layers, per, 12 * d), d)
        lines = full[layers * per:layers * (per + 1)]
        grads.append(lax.dynamic_slice(lines, (0, me * part), (layers, part)))
    else:
        whole = [
            jnp.stack([lax.all_gather(flat[l], "dev", axis=0, tiled=True) for l in range(layers)])
            for flat in flats + (vectors,)
        ]
        line = whole.pop()
        spare = jnp.zeros((layers, BLOCK - 1, 12 * d), bf16)
        block = jnp.concatenate([rows_of(whole, d), line[:, None, :], spare], axis=1)
        down = [(i, (i + n - 1) % n) for i in range(n)]
        tok_up, cot_up = lax.ppermute(tokens, "dev", down), lax.ppermute(cotangent, "dev", down)
        grad, act, act_up, dx, dx_up = compute(
            n, False, ranges, (block,), tokens, cotangent, tok_up, cot_up, layers
        )
        up = [(i, (i + 1) % n) for i in range(n)]
        act = act + lax.ppermute(act_up, "dev", up)
        dx = dx + lax.ppermute(dx_up, "dev", up)
        terms = flats_of(grad[:, :d], d) + [grad[:, d]]
        grads = [
            jnp.stack([
                lax.psum_scatter(term[l].astype(f32), "dev", scatter_dimension=0, tiled=True)
                for l in range(layers)
            ])
            for term in terms
        ]
    return (act.T, dx.T, *grads)


def solution(mesh):
    flat = P(None, "dev")
    rows = P("dev", None)
    return jax.shard_map(
        local,
        mesh=mesh,
        in_specs=(rows, P(), flat, flat, flat, flat, flat, rows),
        out_specs=(rows, rows, flat, flat, flat, flat, flat),
        check_vma=False,
    )
```
